32 devices in a mesh: groups: 2 (over y), adapter: 4 (over z), tensor: 4 (over x, core).
Axes of the slice: x: 2, y: 2, z: 4, core: 2. Of those that a mesh axis runs over, the one named last changes fastest.
Arguments:
- heads_out: bfloat16 [1024, 8192], P(('groups', 'adapter'), 'tensor'), parts along dimension 0, may hold values from -6 to 6
- out_weight: bfloat16 [8192, 8192], P('tensor', 'adapter'), may hold values from -0.0625 to 0.0625
- adapter_ids: int32 [1024], P(('groups', 'adapter')), parts along dimension 0, may hold values from 0 to 31, as said below
- shrink_weight: bfloat16 [64, 64, 8192], P(('groups', 'adapter'), None, 'tensor'), parts along dimension 0, may hold values from -0.0625 to 0.0625
- expand_weight: bfloat16 [64, 64, 8192], P(('groups', 'adapter'), None, 'tensor'), parts along dimension 0, may hold values from -0.75 to 0.75
Outputs:
- mixed: bfloat16 [1024, 8192], P(('groups', 'adapter', 'tensor')), parts along dimension 0
The draws below stay inside these ranges and needn't reach their ends.
There are 2 independent parts, one for each index of `groups`. The reference program is written for one: setup_inputs(seed, part) draws one part's arguments, and reference() takes and returns one part's arrays. A program takes and returns all parts, laid end to end along the dimension named above; an argument that names none is the same for every part. Nothing has to cross between parts.
Inputs may be any that keep to these rules, and one draw needn't show every extreme that they name: `adapter_ids`: among the 128 requests on one index of the adapter axis, at most 32 use adapters held by one owner (adapters k * 8 to (k + 1) * 8 - 1 are held by index k); in every draw one owner gets exactly 32 from every index.
All inputs are finite; a program needn't handle non-finite values.
Results may differ from the reference program's by a relative error of at most 0.0053.
Values may be sent and summed in bfloat16 or wider, within the bound.
A program may use at most 128 MiB of HBM per device.

```python
import jax
import jax.numpy as jnp
from jax import lax

D = 8192
RANK = 64
REQ_DEV = 128
ADP_DEV = 8
TOKENS = 512
ADAPTERS = 32
CAP = 32
N_ADAPTER = 4


def draw_adapter_ids(key, part):
    key = jax.random.fold_in(key, 7)
    owners = N_ADAPTER
    hot = jax.random.randint(jax.random.fold_in(key, 1), (), 0, owners)
    order = jax.vmap(lambda k: jax.random.permutation(k, owners - 1))(jax.random.split(jax.random.fold_in(key, 2), owners))
    place = jnp.arange(REQ_DEV)
    other_slot = jnp.maximum(place - CAP, 0) % (owners - 1)
    others = (hot + 1 + order[:, other_slot]) % owners
    owner = jnp.where(place[None, :] < CAP, hot, others)
    subindex = jax.random.randint(jax.random.fold_in(key, 3), (owners, REQ_DEV), 0, ADP_DEV)
    ident = owner * ADP_DEV + subindex
    mixed_up = jax.vmap(lambda k, b: jax.random.permutation(k, b))(jax.random.split(jax.random.fold_in(key, 4), owners), ident)
    return mixed_up.reshape(owners * REQ_DEV).astype(jnp.int32)


def steps_of(own_key, dims, shards, low, top_value):
    factor_of = 1.0
    for position, blocks in shards:
        draws = jax.random.uniform(jax.random.fold_in(jax.random.fold_in(own_key, 6), position), (blocks,), jnp.float32, low / len(shards), top_value / len(shards))
        factor_of = factor_of * jnp.repeat(jnp.exp(draws), dims[position] // blocks).reshape((-1,) + (1,) * (len(dims) - 1 - position))
    return factor_of


def normal_values(stream_key, dims, width, reach, pieces=(), kind=jnp.bfloat16):
    array = width * jax.random.normal(stream_key, dims, jnp.float32)
    if pieces:
        array = array * steps_of(stream_key, dims, pieces, -0.22, 0.18)
    return jnp.clip(array, -reach, reach).astype(kind)


def setup_inputs(seed: int = 0, part: int = 0) -> dict:
    key_of = jax.random.split(jax.random.key(seed), 6)
    part_keys = jax.random.split(jax.random.fold_in(key_of[5], part), 6)
    heads_out = normal_values(part_keys[0], (TOKENS, D), 1.0, 6.0, ((0, 4), (1, 4)))
    out_weight = normal_values(key_of[1], (D, D), D ** -0.5, 0.0625, ((0, 4), (1, 4)))
    adapter_ids = draw_adapter_ids(jax.random.fold_in(jax.random.fold_in(key_of[5], part), 71), part)
    shrink_weight = normal_values(part_keys[3], (ADAPTERS, RANK, D), D ** -0.5, 0.0625, ((0, 4), (2, 4)))
    expand_weight = normal_values(part_keys[4], (ADAPTERS, RANK, D), RANK ** -0.5, 0.75, ((0, 4), (2, 4)))
    return dict(heads_out=heads_out, out_weight=out_weight, adapter_ids=adapter_ids, shrink_weight=shrink_weight, expand_weight=expand_weight)


def reference(heads_out, out_weight, adapter_ids, shrink_weight, expand_weight):
    base = jnp.dot(heads_out, out_weight, preferred_element_type=jnp.float32).astype(jnp.bfloat16)

    def per_request(item):
        row, ident = item
        shrink = jnp.dot(shrink_weight[ident], row, preferred_element_type=jnp.float32)
        low = (0.5 * shrink).astype(jnp.bfloat16)
        return jnp.dot(low, expand_weight[ident], preferred_element_type=jnp.float32).astype(jnp.bfloat16)

    delta = lax.map(per_request, (heads_out, adapter_ids))
    return (base.astype(jnp.float32) + delta.astype(jnp.float32)).astype(jnp.bfloat16)
```

```python
import functools

import jax
import jax.numpy as jnp
from jax import lax
from jax.experimental import pallas as pl
from jax.experimental.pallas import tpu as pltpu
from jax.sharding import PartitionSpec as P

MESH = pl.DeviceIdType.MESH
F32 = jnp.float32
BF16 = jnp.bfloat16
LANES = 128


def kernel(
    n, tn, cap, rank,
    x_ref, w_ref, s_ref, e_ref, desc_ref, u_ref,
    out_ref,
    xall, w_v, s_v, e_v, desc_v, low_v, psend, precv, dsend, drecv, bsend, brecv, esend, erecv,
    local_sem, xsend_sem, xfwd_sem, xrecv_sem, desc_send, desc_recv, low_send, low_recv,
    p_send, p_recv, d_send, d_recv, b_send, b_recv, e_send, e_recv,
):
    z = lax.axis_index("adapter")
    t = lax.axis_index("tensor")
    rows, width = x_ref.shape
    cols = w_ref.shape[1]
    share = rows // tn
    mids = s_ref.shape[0]
    groups = mids // LANES
    tile = min(512, cols)
    wtile = min(512, width)

    def remote(src, dst, ssem, rsem, **where):
        return pltpu.make_async_remote_copy(
            src_ref=src, dst_ref=dst, send_sem=ssem, recv_sem=rsem, device_id=where, device_id_type=MESH
        )

    def zpeer(j):
        return lax.rem(z + j, n)

    def tpeer(j):
        return lax.rem(t + j, tn)

    x_load = pltpu.make_async_copy(x_ref, xall.at[z], local_sem.at[0])
    s_load = pltpu.make_async_copy(s_ref, s_v, local_sem.at[1])
    w_load = pltpu.make_async_copy(w_ref, w_v, local_sem.at[2])
    e_load = pltpu.make_async_copy(e_ref, e_v, local_sem.at[3])
    x_load.start()
    s_load.start()
    w_load.start()
    e_load.start()

    barrier = pltpu.get_barrier_semaphore()
    for j in range(1, n):
        pl.semaphore_signal(barrier, inc=1, device_id={"adapter": zpeer(j)}, device_id_type=MESH)
    for j in range(1, tn):
        pl.semaphore_signal(barrier, inc=1, device_id={"tensor": tpeer(j)}, device_id_type=MESH)
    desc_v[z] = desc_ref[z]
    pl.semaphore_wait(barrier, n - 1 + tn - 1)

    def desc_copy(j):
        peer = zpeer(j)
        return remote(desc_ref.at[peer], desc_v.at[z], desc_send.at[peer], desc_recv.at[z], adapter=peer)

    for j in range(1, n):
        desc_copy(j).start()

    def own_copy(side):
        return remote(
            x_ref, xall.at[z], xsend_sem.at[side], xrecv_sem.at[z], adapter=z + 1 if side else z - 1
        )

    def fwd_copy(b, peer):
        return remote(xall.at[b], xall.at[b], xfwd_sem.at[b], xrecv_sem.at[b], adapter=peer)

    @pl.when(z + 1 < n)
    def _():
        own_copy(1).start()

    @pl.when(z > 0)
    def _():
        own_copy(0).start()

    def block_of(s):
        m = jnp.minimum(z, n - 1 - z)
        d = (s + 1) // 2
        near = jnp.where(s % 2 == 1, z - d, z + d)
        far = jnp.where(z > n - 1 - z, z - (s - m), z + (s - m))
        return jnp.where(s <= 2 * m, near, far)

    def low_copy(b, j):
        return remote(low_v.at[b, t], low_v.at[b, t], low_send.at[b, j], low_recv.at[b, t], tensor=tpeer(j))

    def part_copy(b, j):
        peer = tpeer(j)
        return remote(psend.at[b, peer], precv.at[b, t], p_send.at[b, j], p_recv.at[b, t], tensor=peer)

    def delta_copy(b):
        return remote(dsend.at[b], drecv.at[z], d_send.at[b], d_recv.at[z], adapter=b)

    def base_copy(b):
        return remote(bsend.at[b], brecv.at[z], b_send.at[b], b_recv.at[z], adapter=b)

    def landed(ref, sem):
        return remote(ref, ref, xsend_sem.at[0], sem, tensor=tpeer(1))

    def mask_of(b):
        kk = desc_v[b, :, pl.ds(rows, LANES)].astype(F32)
        half = lax.broadcasted_iota(jnp.int32, (cap, LANES), 1) // rank
        return [kk == (half + g * (LANES // rank)).astype(F32) for g in range(groups)]

    def first(s):
        b = block_of(s)

        @pl.when(s == 0)
        def _():
            x_load.wait()
            s_load.wait()

        @pl.when(s > 0)
        def _():
            landed(xall.at[b], xrecv_sem.at[b]).wait_recv()

            @pl.when((b < z) & (z + 1 < n))
            def _():
                fwd_copy(b, z + 1).start()

            @pl.when((b > z) & (z > 0))
            def _():
                fwd_copy(b, z - 1).start()

            landed(desc_v.at[b], desc_recv.at[b]).wait_recv()

        picked = jnp.dot(
            desc_v[b, :, pl.ds(0, rows)], xall[b], preferred_element_type=F32
        ).astype(BF16)
        shrunk = lax.dot_general(
            picked, s_v[...], (((1,), (1,)), ((), ())), preferred_element_type=F32
        )
        fold = jnp.zeros((cap, LANES), F32)
        for g, hit in enumerate(mask_of(b)):
            fold = fold + jnp.where(hit, shrunk[:, g * LANES:(g + 1) * LANES], 0.0)
        low_v[b, t] = fold
        for j in range(1, tn):
            low_copy(b, j).start()

        @pl.when(s == 0)
        def _():
            w_load.wait()

        def column(i, carry):
            span = pl.ds(pl.multiple_of(i * tile, tile), tile)
            part = jnp.dot(xall[b], w_v[:, span], preferred_element_type=F32)
            for q in range(tn):
                psend[b, q, :, span] = part[q * share:(q + 1) * share].astype(BF16)
            return carry

        lax.fori_loop(0, cols // tile, column, 0)
        for j in range(1, tn):
            part_copy(b, j).start()

        @pl.when(s == 0)
        def _():
            e_load.wait()

    def second(s):
        b = block_of(s)
        for j in range(1, tn):
            peer = tpeer(j)
            landed(low_v.at[b, peer], low_recv.at[b, peer]).wait_recv()
        total = low_v[b, 0]
        for q in range(1, tn):
            total = total + low_v[b, q]
        low = 0.5 * total
        routed = jnp.concatenate([jnp.where(hit, low, 0.0) for hit in mask_of(b)], axis=1).astype(BF16)
        delta = jnp.dot(routed, e_v[...], preferred_element_type=F32).astype(BF16)

        @pl.when(b == z)
        def _():
            drecv[b] = delta

        @pl.when(b != z)
        def _():
            dsend[b] = delta
            delta_copy(b).start()

        for j in range(1, tn):
            peer = tpeer(j)
            landed(precv.at[b, peer], p_recv.at[b, peer]).wait_recv()
        acc = psend[b, t].astype(F32)
        for j in range(1, tn):
            acc = acc + precv[b, tpeer(j)].astype(F32)
        base = acc.astype(BF16)

        @pl.when(b == z)
        def _():
            brecv[b] = base

        @pl.when(b != z)
        def _():
            bsend[b] = base
            base_copy(b).start()

    def step(s, carry):
        @pl.when(s < n)
        def _():
            first(s)

        @pl.when(s > 0)
        def _():
            second(s - 1)

        return carry

    lax.fori_loop(0, n + 1, step, 0)

    for j in range(1, n):
        peer = zpeer(j)
        landed(drecv.at[peer], d_recv.at[peer]).wait_recv()

    def spread(i, carry):
        span = pl.ds(pl.multiple_of(i * wtile, wtile), wtile)
        flat = drecv[:, :, span].reshape(n * cap, wtile)
        mine = jnp.dot(u_ref[...], flat, preferred_element_type=F32).astype(BF16)
        for q in range(tn):
            esend[q, :, span] = mine[q * share:(q + 1) * share]
        return carry

    lax.fori_loop(0, width // wtile, spread, 0)

    def last_copy(j):
        peer = tpeer(j)
        return remote(esend.at[peer], erecv.at[t], e_send.at[j], e_recv.at[t], tensor=peer)

    for j in range(1, tn):
        last_copy(j).start()
    erecv[t] = esend[t]
    for j in range(1, n):
        peer = zpeer(j)
        landed(brecv.at[peer], b_recv.at[peer]).wait_recv()
    for j in range(1, tn):
        peer = tpeer(j)
        landed(erecv.at[peer], e_recv.at[peer]).wait_recv()
    for o in range(n):
        q, at = (o * cols) // width, (o * cols) % width
        out_ref[:, o * cols:(o + 1) * cols] = (
            brecv[o].astype(F32) + erecv[q, :, at:at + cols].astype(F32)
        ).astype(BF16)

    @pl.when(z + 1 < n)
    def _():
        own_copy(1).wait_send()

    @pl.when(z > 0)
    def _():
        own_copy(0).wait_send()

    def drain(b, carry):
        @pl.when((b < z) & (z + 1 < n))
        def _():
            fwd_copy(b, z + 1).wait_send()

        @pl.when((b > z) & (z > 0))
        def _():
            fwd_copy(b, z - 1).wait_send()

        @pl.when(b != z)
        def _():
            remote(desc_ref.at[b], desc_v.at[z], desc_send.at[b], desc_recv.at[z], adapter=b).wait_send()
            delta_copy(b).wait_send()
            base_copy(b).wait_send()

        for j in range(1, tn):
            low_copy(b, j).wait_send()
            part_copy(b, j).wait_send()
        return carry

    lax.fori_loop(0, n, drain, 0)
    for j in range(1, tn):
        last_copy(j).wait_send()


def local(heads_out, out_weight, adapter_ids, shrink_weight, expand_weight):
    n = lax.axis_size("adapter")
    tn = lax.axis_size("tensor")
    rows, width = heads_out.shape
    local_count, rank = shrink_weight.shape[:2]
    cols = out_weight.shape[1]
    cap = max(2, max(rows // 8, (rows + n - 1) // n))
    mids = local_count * rank
    share = rows // tn

    owner = adapter_ids // local_count
    place = jnp.arange(rows)
    same = (owner[:, None] == owner[None, :]) & (place[None, :] < place[:, None])
    target = owner * cap + jnp.sum(same.astype(jnp.int32), 1)
    hits = target[None, :] == jnp.arange(n * cap)[:, None]
    which = jnp.sum(jnp.where(hits, adapter_ids[None, :] % local_count + 1, 0), 1) - 1
    desc = jnp.concatenate(
        [hits.astype(BF16), jnp.broadcast_to(which[:, None].astype(BF16), (n * cap, LANES))], axis=1
    ).reshape(n, cap, rows + LANES)
    undo = (target[:, None] == jnp.arange(n * cap)[None, :]).astype(BF16)

    any_spec = pl.BlockSpec(memory_space=pl.ANY)
    vmem_spec = pl.BlockSpec(memory_space=pltpu.VMEM)
    dma = pltpu.SemaphoreType.DMA
    return pl.pallas_call(
        functools.partial(kernel, n, tn, cap, rank),
        out_shape=jax.ShapeDtypeStruct((share, n * cols), BF16),
        in_specs=[any_spec] * 4 + [vmem_spec] * 2,
        out_specs=vmem_spec,
        scratch_shapes=[
            pltpu.VMEM((n, rows, width), BF16),
            pltpu.VMEM((width, cols), BF16),
            pltpu.VMEM((mids, width), BF16),
            pltpu.VMEM((mids, width), BF16),
            pltpu.VMEM((n, cap, rows + LANES), BF16),
            pltpu.VMEM((n, tn, cap, LANES), F32),
            pltpu.VMEM((n, tn, share, cols), BF16),
            pltpu.VMEM((n, tn, share, cols), BF16),
            pltpu.VMEM((n, cap, width), BF16),
            pltpu.VMEM((n, cap, width), BF16),
            pltpu.VMEM((n, share, cols), BF16),
            pltpu.VMEM((n, share, cols), BF16),
            pltpu.VMEM((tn, share, width), BF16),
            pltpu.VMEM((tn, share, width), BF16),
            dma((4,)),
            dma((2,)), dma((n,)), dma((n,)),
            dma((n,)), dma((n,)),
            dma((n, tn)), dma((n, tn)),
            dma((n, tn)), dma((n, tn)),
            dma((n,)), dma((n,)),
            dma((n,)), dma((n,)),
            dma((tn,)), dma((tn,)),
        ],
        compiler_params=pltpu.CompilerParams(
            collective_id=0, has_side_effects=True, vmem_limit_bytes=52 * 1024 * 1024
        ),
        cost_estimate=pl.CostEstimate(
            flops=2 * n * rows * width * cols, bytes_accessed=2 * width * (cols + 2 * mids), transcendentals=0
        ),
    )(
        heads_out,
        out_weight,
        shrink_weight.reshape(mids, width),
        expand_weight.reshape(mids, width),
        desc,
        undo,
    )


def solution(mesh):
    placed = (
        P(("groups", "adapter"), "tensor"),
        P("tensor", "adapter"),
        P(("groups", "adapter")),
        P(("groups", "adapter"), None, "tensor"),
        P(("groups", "adapter"), None, "tensor"),
    )
    return jax.shard_map(
        local,
        mesh=mesh,
        in_specs=placed,
        out_specs=P(("groups", "adapter", "tensor"), None),
        check_vma=False,
    )
```

```python
import functools

import jax
import jax.numpy as jnp
from jax import lax
from jax.experimental import pallas as pl
from jax.experimental.pallas import tpu as pltpu
from jax.sharding import PartitionSpec as P

MESH = pl.DeviceIdType.MESH
F32 = jnp.float32
BF16 = jnp.bfloat16
LANES = 128


def kernel(
    n, tn, cap, rank,
    x_ref, w_ref, s_ref, e_ref, desc_ref, u_ref,
    out_ref,
    xall, w_v, s_v, e_v, desc_v, low_v, psend, precv, dsend, drecv, bsend, brecv, esend, erecv,
    local_sem, xsend_sem, xfwd_sem, xrecv_sem, desc_send, desc_recv, low_send, low_recv,
    p_send, p_recv, d_send, d_recv, b_send, b_recv, e_send, e_recv,
):
    z = lax.axis_index("adapter")
    t = lax.axis_index("tensor")
    rows, width = x_ref.shape
    cols = w_ref.shape[1]
    share = rows // tn
    mids = s_ref.shape[0]
    groups = mids // LANES
    tile = min(512, cols)
    wtile = min(512, width)

    def remote(src, dst, ssem, rsem, **where):
        return pltpu.make_async_remote_copy(
            src_ref=src, dst_ref=dst, send_sem=ssem, recv_sem=rsem, device_id=where, device_id_type=MESH
        )

    def zpeer(j):
        return lax.rem(z + j, n)

    def tpeer(j):
        return lax.rem(t + j, tn)

    x_load = pltpu.make_async_copy(x_ref, xall.at[z], local_sem.at[0])
    s_load = pltpu.make_async_copy(s_ref, s_v, local_sem.at[1])
    w_load = pltpu.make_async_copy(w_ref, w_v, local_sem.at[2])
    e_load = pltpu.make_async_copy(e_ref, e_v, local_sem.at[3])
    x_load.start()
    s_load.start()
    w_load.start()
    e_load.start()

    barrier = pltpu.get_barrier_semaphore()
    for j in range(1, n):
        pl.semaphore_signal(barrier, inc=1, device_id={"adapter": zpeer(j)}, device_id_type=MESH)
    for j in range(1, tn):
        pl.semaphore_signal(barrier, inc=1, device_id={"tensor": tpeer(j)}, device_id_type=MESH)
    desc_v[z] = desc_ref[z]
    pl.semaphore_wait(barrier, n - 1 + tn - 1)

    def desc_copy(j):
        peer = zpeer(j)
        return remote(desc_ref.at[peer], desc_v.at[z], desc_send.at[peer], desc_recv.at[z], adapter=peer)

    for j in range(1, n):
        desc_copy(j).start()

    def own_copy(side):
        return remote(
            x_ref, xall.at[z], xsend_sem.at[side], xrecv_sem.at[z], adapter=z + 1 if side else z - 1
        )

    def fwd_copy(b, peer):
        return remote(xall.at[b], xall.at[b], xfwd_sem.at[b], xrecv_sem.at[b], adapter=peer)

    @pl.when(z + 1 < n)
    def _():
        own_copy(1).start()

    @pl.when(z > 0)
    def _():
        own_copy(0).start()

    inner = jnp.where(z > n - 1 - z, -1, 1)
    paired = jnp.minimum(z, n - 1 - z)

    def block_of(s):
        d = (s + 1) // 2
        near = jnp.where(s % 2 == 1, z + inner * d, z - inner * d)
        far = z + inner * (s - paired)
        return jnp.where(s <= 2 * paired, near, far)

    def low_copy(b, j):
        return remote(low_v.at[b, t], low_v.at[b, t], low_send.at[b, j], low_recv.at[b, t], tensor=tpeer(j))

    def part_copy(b, j):
        peer = tpeer(j)
        return remote(psend.at[b, peer], precv.at[b, t], p_send.at[b, j], p_recv.at[b, t], tensor=peer)

    def delta_copy(b):
        return remote(dsend.at[b], drecv.at[z], d_send.at[b], d_recv.at[z], adapter=b)

    def base_copy(b):
        return remote(bsend.at[b], brecv.at[z], b_send.at[b], b_recv.at[z], adapter=b)

    def landed(ref, sem):
        return remote(ref, ref, xsend_sem.at[0], sem, tensor=tpeer(1))

    def mask_of(b):
        kk = desc_v[b, :, pl.ds(rows, LANES)].astype(F32)
        half = lax.broadcasted_iota(jnp.int32, (cap, LANES), 1) // rank
        return [kk == (half + g * (LANES // rank)).astype(F32) for g in range(groups)]

    def take(b):
        landed(xall.at[b], xrecv_sem.at[b]).wait_recv()

        @pl.when((b < z) & (z + 1 < n))
        def _():
            fwd_copy(b, z + 1).start()

        @pl.when((b > z) & (z > 0))
        def _():
            fwd_copy(b, z - 1).start()

    def held(s):
        return (s > 0) & (s <= 2 * paired)

    def first(s):
        b = block_of(s)

        @pl.when(s == 0)
        def _():
            x_load.wait()
            s_load.wait()

        @pl.when(s > 0)
        def _():
            @pl.when((s > 2 * paired) | (s % 2 == 1))
            def _():
                take(b)

            @pl.when((s < 2 * paired) & (s % 2 == 1))
            def _():
                take(block_of(s + 1))

            landed(desc_v.at[b], desc_recv.at[b]).wait_recv()

        picked = jnp.dot(
            desc_v[b, :, pl.ds(0, rows)], xall[b], preferred_element_type=F32
        ).astype(BF16)
        shrunk = lax.dot_general(
            picked, s_v[...], (((1,), (1,)), ((), ())), preferred_element_type=F32
        )
        fold = jnp.zeros((cap, LANES), F32)
        for g, hit in enumerate(mask_of(b)):
            fold = fold + jnp.where(hit, shrunk[:, g * LANES:(g + 1) * LANES], 0.0)
        low_v[b, t] = fold
        for j in range(1, tn):
            low_copy(b, j).start()

        @pl.when(s == 0)
        def _():
            w_load.wait()

        def column(i, carry):
            span = pl.ds(pl.multiple_of(i * tile, tile), tile)
            part = jnp.dot(xall[b], w_v[:, span], preferred_element_type=F32)
            for q in range(tn):
                psend[b, q, :, span] = part[q * share:(q + 1) * share].astype(BF16)
            for j in range(1, tn):
                peer = tpeer(j)
                remote(
                    psend.at[b, peer, :, span], precv.at[b, t, :, span],
                    p_send.at[b, j], p_recv.at[b, t], tensor=peer,
                ).start()
            return carry

        lax.fori_loop(0, cols // tile, column, 0)

        @pl.when(s == 0)
        def _():
            e_load.wait()

    def second(s):
        b = block_of(s)
        for j in range(1, tn):
            peer = tpeer(j)
            landed(low_v.at[b, peer], low_recv.at[b, peer]).wait_recv()
        total = low_v[b, 0]
        for q in range(1, tn):
            total = total + low_v[b, q]
        low = 0.5 * total
        routed = jnp.concatenate([jnp.where(hit, low, 0.0) for hit in mask_of(b)], axis=1).astype(BF16)
        delta = jnp.dot(routed, e_v[...], preferred_element_type=F32).astype(BF16)

        @pl.when(b == z)
        def _():
            drecv[b] = delta

        @pl.when(b != z)
        def _():
            dsend[b] = delta

        @pl.when((b != z) & jnp.logical_not(held(s)))
        def _():
            delta_copy(b).start()

        for j in range(1, tn):
            peer = tpeer(j)
            landed(precv.at[b, peer], p_recv.at[b, peer]).wait_recv()
        acc = psend[b, t].astype(F32)
        for j in range(1, tn):
            acc = acc + precv[b, tpeer(j)].astype(F32)
        base = acc.astype(BF16)

        @pl.when(b == z)
        def _():
            brecv[b] = base

        @pl.when(b != z)
        def _():
            bsend[b] = base

        @pl.when((b != z) & jnp.logical_not(held(s)))
        def _():
            base_copy(b).start()

    def step(s, carry):
        @pl.when(s < n)
        def _():
            first(s)

        @pl.when((s == max(n - 1, 3)) & (paired > 0))
        def _():
            release(1)

        @pl.when(s > 0)
        def _():
            second(s - 1)

        return carry

    def release(s):
        b = block_of(s)
        delta_copy(b).start()
        base_copy(b).start()

    def release_all(s, carry):
        @pl.when(held(s) & (s > 1))
        def _():
            release(s)

        return carry

    lax.fori_loop(0, n + 1, step, 0)
    lax.fori_loop(2, n, release_all, 0)

    for j in range(1, n):
        peer = zpeer(j)
        landed(drecv.at[peer], d_recv.at[peer]).wait_recv()

    def spread(i, carry):
        span = pl.ds(pl.multiple_of(i * wtile, wtile), wtile)
        flat = drecv[:, :, span].reshape(n * cap, wtile)
        mine = jnp.dot(u_ref[...], flat, preferred_element_type=F32).astype(BF16)
        for q in range(tn):
            esend[q, :, span] = mine[q * share:(q + 1) * share]
        return carry

    lax.fori_loop(0, width // wtile, spread, 0)

    def last_copy(j):
        peer = tpeer(j)
        return remote(esend.at[peer], erecv.at[t], e_send.at[j], e_recv.at[t], tensor=peer)

    for j in range(1, tn):
        last_copy(j).start()
    erecv[t] = esend[t]
    for j in range(1, n):
        peer = zpeer(j)
        landed(brecv.at[peer], b_recv.at[peer]).wait_recv()
    for j in range(1, tn):
        peer = tpeer(j)
        landed(erecv.at[peer], e_recv.at[peer]).wait_recv()
    for o in range(n):
        q, at = (o * cols) // width, (o * cols) % width
        out_ref[:, o * cols:(o + 1) * cols] = (
            brecv[o].astype(F32) + erecv[q, :, at:at + cols].astype(F32)
        ).astype(BF16)

    @pl.when(z + 1 < n)
    def _():
        own_copy(1).wait_send()

    @pl.when(z > 0)
    def _():
        own_copy(0).wait_send()

    def drain(b, carry):
        @pl.when((b < z) & (z + 1 < n))
        def _():
            fwd_copy(b, z + 1).wait_send()

        @pl.when((b > z) & (z > 0))
        def _():
            fwd_copy(b, z - 1).wait_send()

        @pl.when(b != z)
        def _():
            remote(desc_ref.at[b], desc_v.at[z], desc_send.at[b], desc_recv.at[z], adapter=b).wait_send()
            delta_copy(b).wait_send()
            base_copy(b).wait_send()

        for j in range(1, tn):
            low_copy(b, j).wait_send()
            part_copy(b, j).wait_send()
        return carry

    lax.fori_loop(0, n, drain, 0)
    for j in range(1, tn):
        last_copy(j).wait_send()


def local(heads_out, out_weight, adapter_ids, shrink_weight, expand_weight):
    n = lax.axis_size("adapter")
    tn = lax.axis_size("tensor")
    rows, width = heads_out.shape
    local_count, rank = shrink_weight.shape[:2]
    cols = out_weight.shape[1]
    cap = max(2, max(rows // 8, (rows + n - 1) // n))
    mids = local_count * rank
    share = rows // tn

    owner = adapter_ids // local_count
    place = jnp.arange(rows)
    same = (owner[:, None] == owner[None, :]) & (place[None, :] < place[:, None])
    target = owner * cap + jnp.sum(same.astype(jnp.int32), 1)
    hits = target[None, :] == jnp.arange(n * cap)[:, None]
    which = jnp.sum(jnp.where(hits, adapter_ids[None, :] % local_count + 1, 0), 1) - 1
    desc = jnp.concatenate(
        [hits.astype(BF16), jnp.broadcast_to(which[:, None].astype(BF16), (n * cap, LANES))], axis=1
    ).reshape(n, cap, rows + LANES)
    undo = (target[:, None] == jnp.arange(n * cap)[None, :]).astype(BF16)

    any_spec = pl.BlockSpec(memory_space=pl.ANY)
    vmem_spec = pl.BlockSpec(memory_space=pltpu.VMEM)
    dma = pltpu.SemaphoreType.DMA
    return pl.pallas_call(
        functools.partial(kernel, n, tn, cap, rank),
        out_shape=jax.ShapeDtypeStruct((share, n * cols), BF16),
        in_specs=[any_spec] * 4 + [vmem_spec] * 2,
        out_specs=vmem_spec,
        scratch_shapes=[
            pltpu.VMEM((n, rows, width), BF16),
            pltpu.VMEM((width, cols), BF16),
            pltpu.VMEM((mids, width), BF16),
            pltpu.VMEM((mids, width), BF16),
            pltpu.VMEM((n, cap, rows + LANES), BF16),
            pltpu.VMEM((n, tn, cap, LANES), F32),
            pltpu.VMEM((n, tn, share, cols), BF16),
            pltpu.VMEM((n, tn, share, cols), BF16),
            pltpu.VMEM((n, cap, width), BF16),
            pltpu.VMEM((n, cap, width), BF16),
            pltpu.VMEM((n, share, cols), BF16),
            pltpu.VMEM((n, share, cols), BF16),
            pltpu.VMEM((tn, share, width), BF16),
            pltpu.VMEM((tn, share, width), BF16),
            dma((4,)),
            dma((2,)), dma((n,)), dma((n,)),
            dma((n,)), dma((n,)),
            dma((n, tn)), dma((n, tn)),
            dma((n, tn)), dma((n, tn)),
            dma((n,)), dma((n,)),
            dma((n,)), dma((n,)),
            dma((tn,)), dma((tn,)),
        ],
        compiler_params=pltpu.CompilerParams(
            collective_id=0, has_side_effects=True, vmem_limit_bytes=52 * 1024 * 1024
        ),
        cost_estimate=pl.CostEstimate(
            flops=2 * n * rows * width * cols, bytes_accessed=2 * width * (cols + 2 * mids), transcendentals=0
        ),
    )(
        heads_out,
        out_weight,
        shrink_weight.reshape(mids, width),
        expand_weight.reshape(mids, width),
        desc,
        undo,
    )


def solution(mesh):
    placed = (
        P(("groups", "adapter"), "tensor"),
        P("tensor", "adapter"),
        P(("groups", "adapter")),
        P(("groups", "adapter"), None, "tensor"),
        P(("groups", "adapter"), None, "tensor"),
    )
    return jax.shard_map(
        local,
        mesh=mesh,
        in_specs=placed,
        out_specs=P(("groups", "adapter", "tensor"), None),
        check_vma=False,
    )
```

```python
import functools

import jax
import jax.numpy as jnp
from jax import lax
from jax.experimental import pallas as pl
from jax.experimental.pallas import tpu as pltpu
from jax.sharding import PartitionSpec as P

MESH = pl.DeviceIdType.MESH
F32 = jnp.float32
BF16 = jnp.bfloat16
LANES = 128
PIECES = 2


def kernel(
    n, tn, cap, rank, count,
    x_ref, w_ref, s_ref, e_ref, ids_ref,
    out_ref,
    xall, w_v, s_v, e_v, desc_ref, undo, desc_v, low_v, psend, precv, dsend, drecv, bsend, brecv, esend, erecv,
    local_sem, xsend_sem, xfwd_sem, xrecv_sem, desc_send, desc_recv, low_send, low_recv,
    p_send, p_recv, d_send, d_recv, b_send, b_recv, e_send, e_recv,
):
    z = lax.axis_index("adapter")
    t = lax.axis_index("tensor")
    rows, width = x_ref.shape
    cols = w_ref.shape[1]
    share = rows // tn
    mids = s_ref.shape[0]
    groups = mids // LANES
    tile = min(512, cols)
    wtile = min(512, width)

    def remote(src, dst, ssem, rsem, **where):
        return pltpu.make_async_remote_copy(
            src_ref=src, dst_ref=dst, send_sem=ssem, recv_sem=rsem, device_id=where, device_id_type=MESH
        )

    def zpeer(j):
        return lax.rem(z + j, n)

    def tpeer(j):
        return lax.rem(t + j, tn)

    x_load = pltpu.make_async_copy(x_ref, xall.at[z], local_sem.at[0])
    s_load = pltpu.make_async_copy(s_ref, s_v, local_sem.at[1])
    w_load = pltpu.make_async_copy(w_ref, w_v, local_sem.at[2])
    e_load = pltpu.make_async_copy(e_ref, e_v, local_sem.at[3])
    x_load.start()
    s_load.start()
    w_load.start()
    e_load.start()

    barrier = pltpu.get_barrier_semaphore()
    for j in range(1, n):
        pl.semaphore_signal(barrier, inc=1, device_id={"adapter": zpeer(j)}, device_id_type=MESH)
    for j in range(1, tn):
        pl.semaphore_signal(barrier, inc=1, device_id={"tensor": tpeer(j)}, device_id_type=MESH)
    pl.semaphore_wait(barrier, n - 1 + tn - 1)

    def desc_copy(j):
        peer = zpeer(j)
        return remote(desc_ref.at[peer], desc_v.at[z], desc_send.at[peer], desc_recv.at[z], adapter=peer)

    piece = rows // PIECES

    def own_copy(side, h):
        part = pl.ds(h * piece, piece)
        return remote(
            x_ref.at[part], xall.at[z, part], xsend_sem.at[side, h], xrecv_sem.at[z, h],
            adapter=z + 1 if side else z - 1,
        )

    def fwd_copy(b, h, peer):
        part = pl.ds(h * piece, piece)
        return remote(xall.at[b, part], xall.at[b, part], xfwd_sem.at[b, h], xrecv_sem.at[b, h], adapter=peer)

    for h in range(PIECES):
        @pl.when(z + 1 < n)
        def _():
            own_copy(1, h).start()

        @pl.when(z > 0)
        def _():
            own_copy(0, h).start()

    ids = jnp.broadcast_to(ids_ref[...], (rows, rows))
    owner = jnp.zeros((rows, rows), jnp.int32)
    for o in range(1, n):
        owner = owner + (ids >= o * count).astype(jnp.int32)
    at = lax.broadcasted_iota(jnp.int32, (rows, rows), 0)
    lane = lax.broadcasted_iota(jnp.int32, (rows, rows), 1)
    owner_of = owner.astype(F32).T.astype(jnp.int32)
    place = jnp.sum(((owner == owner_of) & (at < lane)).astype(F32), axis=0, keepdims=True)
    target = owner[:1] * cap + place.astype(jnp.int32)
    slots = n * cap
    hits = jnp.broadcast_to(target, (slots, rows)) == lax.broadcasted_iota(jnp.int32, (slots, rows), 0)
    inside = (ids[:1] - owner[:1] * count + 1).astype(F32)
    which = jnp.sum(jnp.where(hits, jnp.broadcast_to(inside, (slots, rows)), 0.0), axis=1, keepdims=True) - 1.0
    table = hits.astype(F32)
    undo[...] = table.T.astype(BF16)
    desc_ref[:, :, pl.ds(0, rows)] = table.astype(BF16).reshape(n, cap, rows)
    desc_ref[:, :, pl.ds(rows, LANES)] = (
        jnp.broadcast_to(which, (slots, LANES)).astype(BF16).reshape(n, cap, LANES)
    )
    for j in range(1, n):
        desc_copy(j).start()
    desc_v[z] = desc_ref[z]

    inner = jnp.where(z > n - 1 - z, -1, 1)
    paired = jnp.minimum(z, n - 1 - z)

    def block_of(s):
        d = (s + 1) // 2
        near = jnp.where(s % 2 == 1, z + inner * d, z - inner * d)
        far = z + inner * (s - paired)
        return jnp.where(s <= 2 * paired, near, far)

    def low_copy(b, j):
        return remote(low_v.at[b, t], low_v.at[b, t], low_send.at[b, j], low_recv.at[b, t], tensor=tpeer(j))

    def part_copy(b, j):
        peer = tpeer(j)
        return remote(psend.at[b, peer], precv.at[b, t], p_send.at[b, j], p_recv.at[b, t], tensor=peer)

    def delta_copy(b):
        return remote(dsend.at[b], drecv.at[z], d_send.at[b], d_recv.at[z], adapter=b)

    def base_copy(b):
        return remote(bsend.at[b], brecv.at[z], b_send.at[b], b_recv.at[z], adapter=b)

    def landed(ref, sem):
        return remote(ref, ref, local_sem.at[4], sem, tensor=tpeer(1))

    def mask_of(b):
        kk = desc_v[b, :, pl.ds(rows, LANES)].astype(F32)
        half = lax.broadcasted_iota(jnp.int32, (cap, LANES), 1) // rank
        return [kk == (half + g * (LANES // rank)).astype(F32) for g in range(groups)]

    def take(b, h):
        part = xall.at[b, pl.ds(h * piece, piece)]
        landed(part, xrecv_sem.at[b, h]).wait_recv()

        @pl.when((b < z) & (z + 1 < n))
        def _():
            fwd_copy(b, h, z + 1).start()

        @pl.when((b > z) & (z > 0))
        def _():
            fwd_copy(b, h, z - 1).start()

    def held(s):
        return (s > 0) & (s <= 2 * paired)

    def first(s):
        b = block_of(s)

        @pl.when(s == 0)
        def _():
            x_load.wait()
            s_load.wait()

        @pl.when(s > 0)
        def _():
            for h in range(PIECES):
                @pl.when((s > 2 * paired) | (s % 2 == 1))
                def _():
                    take(b, h)

                @pl.when((s < 2 * paired) & (s % 2 == 1))
                def _():
                    take(block_of(s + 1), h)

            landed(desc_v.at[b], desc_recv.at[b]).wait_recv()

        picked = jnp.dot(
            desc_v[b, :, pl.ds(0, rows)], xall[b], preferred_element_type=F32
        ).astype(BF16)
        shrunk = lax.dot_general(
            picked, s_v[...], (((1,), (1,)), ((), ())), preferred_element_type=F32
        )
        fold = jnp.zeros((cap, LANES), F32)
        for g, hit in enumerate(mask_of(b)):
            fold = fold + jnp.where(hit, shrunk[:, g * LANES:(g + 1) * LANES], 0.0)
        low_v[b, t] = fold
        for j in range(1, tn):
            low_copy(b, j).start()

        @pl.when(s == 0)
        def _():
            w_load.wait()

        def column(i, carry):
            span = pl.ds(pl.multiple_of(i * tile, tile), tile)
            part = jnp.dot(xall[b], w_v[:, span], preferred_element_type=F32)
            for q in range(tn):
                psend[b, q, :, span] = part[q * share:(q + 1) * share].astype(BF16)
            for j in range(1, tn):
                peer = tpeer(j)
                remote(
                    psend.at[b, peer, :, span], precv.at[b, t, :, span],
                    p_send.at[b, j], p_recv.at[b, t], tensor=peer,
                ).start()
            return carry

        lax.fori_loop(0, cols // tile, column, 0)

        @pl.when(s == 0)
        def _():
            e_load.wait()

    def delta_part(s):
        b = block_of(s)
        for j in range(1, tn):
            peer = tpeer(j)
            landed(low_v.at[b, peer], low_recv.at[b, peer]).wait_recv()
        total = low_v[b, 0]
        for q in range(1, tn):
            total = total + low_v[b, q]
        low = 0.5 * total
        routed = jnp.concatenate([jnp.where(hit, low, 0.0) for hit in mask_of(b)], axis=1).astype(BF16)
        delta = jnp.dot(routed, e_v[...], preferred_element_type=F32).astype(BF16)

        @pl.when(b == z)
        def _():
            drecv[b] = delta

        @pl.when(b != z)
        def _():
            dsend[b] = delta

        @pl.when((b != z) & jnp.logical_not(held(s)))
        def _():
            delta_copy(b).start()

    def base_part(s):
        b = block_of(s)
        for j in range(1, tn):
            peer = tpeer(j)
            landed(precv.at[b, peer], p_recv.at[b, peer]).wait_recv()
        acc = psend[b, t].astype(F32)
        for j in range(1, tn):
            acc = acc + precv[b, tpeer(j)].astype(F32)
        base = acc.astype(BF16)

        @pl.when(b == z)
        def _():
            brecv[b] = base

        @pl.when(b != z)
        def _():
            bsend[b] = base

        @pl.when((b != z) & jnp.logical_not(held(s)))
        def _():
            base_copy(b).start()

    last = max(n - 1, 3)

    def step(s, carry):
        @pl.when(s < n)
        def _():
            first(s)

        @pl.when((s == last) & (paired > 0))
        def _():
            delta_copy(block_of(1)).start()

        @pl.when(s < n)
        def _():
            delta_part(s)

        @pl.when((s == last) & (paired > 0))
        def _():
            delta_copy(block_of(2)).start()
            base_copy(block_of(1)).start()

        @pl.when(s > 0)
        def _():
            base_part(s - 1)

        return carry

    def release_all(s, carry):
        @pl.when(held(s))
        def _():
            @pl.when(s > 2)
            def _():
                delta_copy(block_of(s)).start()

            @pl.when(s > 1)
            def _():
                base_copy(block_of(s)).start()

        return carry

    lax.fori_loop(0, n + 1, step, 0)
    lax.fori_loop(2, n, release_all, 0)

    for j in range(1, n):
        peer = zpeer(j)
        landed(drecv.at[peer], d_recv.at[peer]).wait_recv()

    def spread(i, carry):
        span = pl.ds(pl.multiple_of(i * wtile, wtile), wtile)
        flat = drecv[:, :, span].reshape(n * cap, wtile)
        mine = jnp.dot(undo[...], flat, preferred_element_type=F32).astype(BF16)
        for q in range(tn):
            esend[q, :, span] = mine[q * share:(q + 1) * share]
        return carry

    lax.fori_loop(0, width // wtile, spread, 0)

    def last_copy(j):
        peer = tpeer(j)
        return remote(esend.at[peer], erecv.at[t], e_send.at[j], e_recv.at[t], tensor=peer)

    for j in range(1, tn):
        last_copy(j).start()
    erecv[t] = esend[t]
    for j in range(1, n):
        peer = zpeer(j)
        landed(brecv.at[peer], b_recv.at[peer]).wait_recv()
    for j in range(1, tn):
        peer = tpeer(j)
        landed(erecv.at[peer], e_recv.at[peer]).wait_recv()
    for o in range(n):
        q, at = (o * cols) // width, (o * cols) % width
        out_ref[:, o * cols:(o + 1) * cols] = (
            brecv[o].astype(F32) + erecv[q, :, at:at + cols].astype(F32)
        ).astype(BF16)

    for h in range(PIECES):
        @pl.when(z + 1 < n)
        def _():
            own_copy(1, h).wait_send()

        @pl.when(z > 0)
        def _():
            own_copy(0, h).wait_send()

    def drain(b, carry):
        for h in range(PIECES):
            @pl.when((b < z) & (z + 1 < n))
            def _():
                fwd_copy(b, h, z + 1).wait_send()

            @pl.when((b > z) & (z > 0))
            def _():
                fwd_copy(b, h, z - 1).wait_send()

        @pl.when(b != z)
        def _():
            remote(desc_ref.at[b], desc_v.at[z], desc_send.at[b], desc_recv.at[z], adapter=b).wait_send()
            delta_copy(b).wait_send()
            base_copy(b).wait_send()

        for j in range(1, tn):
            low_copy(b, j).wait_send()
            part_copy(b, j).wait_send()
        return carry

    lax.fori_loop(0, n, drain, 0)
    for j in range(1, tn):
        last_copy(j).wait_send()


def local(heads_out, out_weight, adapter_ids, shrink_weight, expand_weight):
    n = lax.axis_size("adapter")
    tn = lax.axis_size("tensor")
    rows, width = heads_out.shape
    local_count, rank = shrink_weight.shape[:2]
    cols = out_weight.shape[1]
    cap = max(2, max(rows // 8, (rows + n - 1) // n))
    mids = local_count * rank
    share = rows // tn

    any_spec = pl.BlockSpec(memory_space=pltpu.HBM)
    vmem_spec = pl.BlockSpec(memory_space=pltpu.VMEM)
    dma = pltpu.SemaphoreType.DMA
    return pl.pallas_call(
        functools.partial(kernel, n, tn, cap, rank, local_count),
        out_shape=jax.ShapeDtypeStruct((share, n * cols), BF16),
        in_specs=[any_spec] * 4 + [vmem_spec],
        out_specs=vmem_spec,
        scratch_shapes=[
            pltpu.VMEM((n, rows, width), BF16),
            pltpu.VMEM((width, cols), BF16),
            pltpu.VMEM((mids, width), BF16),
            pltpu.VMEM((mids, width), BF16),
            pltpu.VMEM((n, cap, rows + LANES), BF16),
            pltpu.VMEM((rows, n * cap), BF16),
            pltpu.VMEM((n, cap, rows + LANES), BF16),
            pltpu.VMEM((n, tn, cap, LANES), F32),
            pltpu.VMEM((n, tn, share, cols), BF16),
            pltpu.VMEM((n, tn, share, cols), BF16),
            pltpu.VMEM((n, cap, width), BF16),
            pltpu.VMEM((n, cap, width), BF16),
            pltpu.VMEM((n, share, cols), BF16),
            pltpu.VMEM((n, share, cols), BF16),
            pltpu.VMEM((tn, share, width), BF16),
            pltpu.VMEM((tn, share, width), BF16),
            dma((5,)),
            dma((2, PIECES)), dma((n, PIECES)), dma((n, PIECES)),
            dma((n,)), dma((n,)),
            dma((n, tn)), dma((n, tn)),
            dma((n, tn)), dma((n, tn)),
            dma((n,)), dma((n,)),
            dma((n,)), dma((n,)),
            dma((tn,)), dma((tn,)),
        ],
        compiler_params=pltpu.CompilerParams(
            collective_id=0, has_side_effects=True, vmem_limit_bytes=52 * 1024 * 1024
        ),
        cost_estimate=pl.CostEstimate(
            flops=2 * n * rows * width * cols, bytes_accessed=2 * width * (cols + 2 * mids), transcendentals=0
        ),
    )(
        heads_out,
        out_weight,
        shrink_weight.reshape(mids, width),
        expand_weight.reshape(mids, width),
        adapter_ids.reshape(1, rows),
    )


def solution(mesh):
    placed = (
        P(("groups", "adapter"), "tensor"),
        P("tensor", "adapter"),
        P(("groups", "adapter")),
        P(("groups", "adapter"), None, "tensor"),
        P(("groups", "adapter"), None, "tensor"),
    )
    return jax.shard_map(
        local,
        mesh=mesh,
        in_specs=placed,
        out_specs=P(("groups", "adapter", "tensor"), None),
        check_vma=False,
    )
```

```python
import functools

import jax
import jax.numpy as jnp
from jax import lax
from jax.experimental import pallas as pl
from jax.experimental.pallas import tpu as pltpu
from jax.sharding import PartitionSpec as P

MESH = pl.DeviceIdType.MESH
F32 = jnp.float32
BF16 = jnp.bfloat16
LANES = 128
PIECES = 2


def kernel(
    n, tn, cap, rank, count,
    x_ref, w_ref, s_ref, e_ref, ids_ref,
    out_ref,
    xall, w_v, s_v, e_v, desc_ref, undo, desc_v, low_v, psend, precv, dsend, drecv, bsend, brecv, esend, erecv,
    local_sem, xsend_sem, xfwd_sem, xrecv_sem, desc_send, desc_recv, low_send, low_recv,
    p_send, p_recv, d_send, d_recv, b_send, b_recv, e_send, e_recv,
):
    z = lax.axis_index("adapter")
    t = lax.axis_index("tensor")
    rows, width = x_ref.shape
    cols = w_ref.shape[1]
    share = rows // tn
    mids = s_ref.shape[0]
    groups = mids // LANES
    tile = min(512, cols)
    wtile = min(512, width)

    def remote(src, dst, ssem, rsem, **where):
        return pltpu.make_async_remote_copy(
            src_ref=src, dst_ref=dst, send_sem=ssem, recv_sem=rsem, device_id=where, device_id_type=MESH
        )

    def zpeer(j):
        return lax.rem(z + j, n)

    def tpeer(j):
        return lax.rem(t + j, tn)

    x_load = pltpu.make_async_copy(x_ref, xall.at[z], local_sem.at[0])
    s_load = pltpu.make_async_copy(s_ref, s_v, local_sem.at[1])
    w_load = pltpu.make_async_copy(w_ref, w_v, local_sem.at[2])
    e_load = pltpu.make_async_copy(e_ref, e_v, local_sem.at[3])
    x_load.start()
    s_load.start()
    w_load.start()
    e_load.start()

    barrier = pltpu.get_barrier_semaphore()
    for j in range(1, n):
        pl.semaphore_signal(barrier, inc=1, device_id={"adapter": zpeer(j)}, device_id_type=MESH)
    for j in range(1, tn):
        pl.semaphore_signal(barrier, inc=1, device_id={"tensor": tpeer(j)}, device_id_type=MESH)
    pl.semaphore_wait(barrier, n - 1 + tn - 1)

    def desc_copy(j):
        peer = zpeer(j)
        return remote(desc_ref.at[peer], desc_v.at[z], desc_send.at[peer], desc_recv.at[z], adapter=peer)

    piece = rows // PIECES

    def own_copy(side, h):
        part = pl.ds(h * piece, piece)
        return remote(
            x_ref.at[part], xall.at[z, part], xsend_sem.at[side, h], xrecv_sem.at[z, h],
            adapter=z + 1 if side else z - 1,
        )

    def fwd_copy(b, h, peer):
        part = pl.ds(h * piece, piece)
        return remote(xall.at[b, part], xall.at[b, part], xfwd_sem.at[b, h], xrecv_sem.at[b, h], adapter=peer)

    for h in range(PIECES):
        @pl.when(z + 1 < n)
        def _():
            own_copy(1, h).start()

        @pl.when(z > 0)
        def _():
            own_copy(0, h).start()

    ids = jnp.broadcast_to(ids_ref[...], (rows, rows))
    owner = jnp.zeros((rows, rows), jnp.int32)
    for o in range(1, n):
        owner = owner + (ids >= o * count).astype(jnp.int32)
    at = lax.broadcasted_iota(jnp.int32, (rows, rows), 0)
    lane = lax.broadcasted_iota(jnp.int32, (rows, rows), 1)
    owner_of = owner.astype(F32).T.astype(jnp.int32)
    place = jnp.sum(((owner == owner_of) & (at < lane)).astype(F32), axis=0, keepdims=True)
    target = owner[:1] * cap + place.astype(jnp.int32)
    slots = n * cap
    hits = jnp.broadcast_to(target, (slots, rows)) == lax.broadcasted_iota(jnp.int32, (slots, rows), 0)
    inside = (ids[:1] - owner[:1] * count + 1).astype(F32)
    which = jnp.sum(jnp.where(hits, jnp.broadcast_to(inside, (slots, rows)), 0.0), axis=1, keepdims=True) - 1.0
    table = hits.astype(F32)
    undo[...] = table.T.astype(BF16)
    desc_ref[:, :, pl.ds(0, rows)] = table.astype(BF16).reshape(n, cap, rows)
    desc_ref[:, :, pl.ds(rows, LANES)] = (
        jnp.broadcast_to(which, (slots, LANES)).astype(BF16).reshape(n, cap, LANES)
    )
    for j in range(1, n):
        desc_copy(j).start()
    desc_v[z] = desc_ref[z]

    inner = jnp.where(z > n - 1 - z, -1, 1)
    paired = jnp.minimum(z, n - 1 - z)

    def block_of(s):
        d = (s + 1) // 2
        near = jnp.where(s % 2 == 1, z + inner * d, z - inner * d)
        far = z + inner * (s - paired)
        return jnp.where(s <= 2 * paired, near, far)

    def low_copy(b, j):
        return remote(low_v.at[b, t], low_v.at[b, t], low_send.at[b, j], low_recv.at[b, t], tensor=tpeer(j))

    def part_copy(b, j):
        peer = tpeer(j)
        return remote(psend.at[b, peer], precv.at[b, t], p_send.at[b, j], p_recv.at[b, t], tensor=peer)

    def delta_copy(b):
        return remote(dsend.at[b], drecv.at[z], d_send.at[b], d_recv.at[z], adapter=b)

    def base_copy(b):
        return remote(bsend.at[b], brecv.at[z], b_send.at[b], b_recv.at[z], adapter=b)

    def landed(ref, sem):
        return remote(ref, ref, local_sem.at[4], sem, tensor=tpeer(1))

    def mask_of(b):
        kk = desc_v[b, :, pl.ds(rows, LANES)].astype(F32)
        half = lax.broadcasted_iota(jnp.int32, (cap, LANES), 1) // rank
        return [kk == (half + g * (LANES // rank)).astype(F32) for g in range(groups)]

    def take(b, h):
        part = xall.at[b, pl.ds(h * piece, piece)]
        landed(part, xrecv_sem.at[b, h]).wait_recv()

        @pl.when((b < z) & (z + 1 < n))
        def _():
            fwd_copy(b, h, z + 1).start()

        @pl.when((b > z) & (z > 0))
        def _():
            fwd_copy(b, h, z - 1).start()

    def held(s):
        return (s > 0) & (s <= 2 * paired)

    def first(s):
        b = block_of(s)

        @pl.when(s == 0)
        def _():
            x_load.wait()
            s_load.wait()

        @pl.when(s > 0)
        def _():
            for h in range(PIECES):
                @pl.when((s > 2 * paired) | (s % 2 == 1))
                def _():
                    take(b, h)

                @pl.when((s < 2 * paired) & (s % 2 == 1))
                def _():
                    take(block_of(s + 1), h)

            landed(desc_v.at[b], desc_recv.at[b]).wait_recv()

        picked = jnp.dot(
            desc_v[b, :, pl.ds(0, rows)], xall[b], preferred_element_type=F32
        ).astype(BF16)
        shrunk = lax.dot_general(
            picked, s_v[...], (((1,), (1,)), ((), ())), preferred_element_type=F32
        )
        fold = jnp.zeros((cap, LANES), F32)
        for g, hit in enumerate(mask_of(b)):
            fold = fold + jnp.where(hit, shrunk[:, g * LANES:(g + 1) * LANES], 0.0)
        low_v[b, t] = fold
        for j in range(1, tn):
            low_copy(b, j).start()

        @pl.when(s == 0)
        def _():
            w_load.wait()

        def column(i, carry):
            span = pl.ds(pl.multiple_of(i * tile, tile), tile)
            part = jnp.dot(xall[b], w_v[:, span], preferred_element_type=F32)
            for q in range(tn):
                psend[b, q, :, span] = part[q * share:(q + 1) * share].astype(BF16)
            for j in range(1, tn):
                peer = tpeer(j)
                remote(
                    psend.at[b, peer, :, span], precv.at[b, t, :, span],
                    p_send.at[b, j], p_recv.at[b, t], tensor=peer,
                ).start()
            return carry

        lax.fori_loop(0, cols // tile, column, 0)

        @pl.when(s == 0)
        def _():
            e_load.wait()

    def delta_part(s):
        b = block_of(s)
        for j in range(1, tn):
            peer = tpeer(j)
            landed(low_v.at[b, peer], low_recv.at[b, peer]).wait_recv()
        total = low_v[b, 0]
        for q in range(1, tn):
            total = total + low_v[b, q]
        low = 0.5 * total
        routed = jnp.concatenate([jnp.where(hit, low, 0.0) for hit in mask_of(b)], axis=1).astype(BF16)
        delta = jnp.dot(routed, e_v[...], preferred_element_type=F32).astype(BF16)

        @pl.when(b == z)
        def _():
            drecv[b] = delta

        @pl.when(b != z)
        def _():
            dsend[b] = delta

        @pl.when((b != z) & jnp.logical_not(held(s)))
        def _():
            delta_copy(b).start()

    def base_part(s):
        b = block_of(s)
        for j in range(1, tn):
            peer = tpeer(j)
            landed(precv.at[b, peer], p_recv.at[b, peer]).wait_recv()
        acc = psend[b, t].astype(F32)
        for j in range(1, tn):
            acc = acc + precv[b, tpeer(j)].astype(F32)
        base = acc.astype(BF16)

        @pl.when(b == z)
        def _():
            brecv[b] = base

        @pl.when(b != z)
        def _():
            bsend[b] = base

        @pl.when((b != z) & jnp.logical_not(held(s)))
        def _():
            base_copy(b).start()

    last = max(n - 1, 3)

    def step(s, carry):
        @pl.when(s < n)
        def _():
            first(s)

        @pl.when((s == last) & (paired > 0))
        def _():
            delta_copy(block_of(1)).start()
            delta_copy(block_of(2)).start()
            base_copy(block_of(1)).start()

        @pl.when(s < n)
        def _():
            delta_part(s)

        @pl.when(s > 0)
        def _():
            base_part(s - 1)

        return carry

    def release_all(s, carry):
        @pl.when(held(s))
        def _():
            @pl.when(s > 2)
            def _():
                delta_copy(block_of(s)).start()

            @pl.when(s > 1)
            def _():
                base_copy(block_of(s)).start()

        return carry

    lax.fori_loop(0, n + 1, step, 0)
    lax.fori_loop(2, n, release_all, 0)

    for j in range(1, n):
        peer = zpeer(j)
        landed(drecv.at[peer], d_recv.at[peer]).wait_recv()

    def spread(i, carry):
        span = pl.ds(pl.multiple_of(i * wtile, wtile), wtile)
        flat = drecv[:, :, span].reshape(n * cap, wtile)
        mine = jnp.dot(undo[...], flat, preferred_element_type=F32).astype(BF16)
        for q in range(tn):
            esend[q, :, span] = mine[q * share:(q + 1) * share]
        return carry

    lax.fori_loop(0, width // wtile, spread, 0)

    def last_copy(j):
        peer = tpeer(j)
        return remote(esend.at[peer], erecv.at[t], e_send.at[j], e_recv.at[t], tensor=peer)

    for j in range(1, tn):
        last_copy(j).start()
    erecv[t] = esend[t]
    for j in range(1, n):
        peer = zpeer(j)
        landed(brecv.at[peer], b_recv.at[peer]).wait_recv()
    for j in range(1, tn):
        peer = tpeer(j)
        landed(erecv.at[peer], e_recv.at[peer]).wait_recv()
    for o in range(n):
        q, at = (o * cols) // width, (o * cols) % width
        out_ref[:, o * cols:(o + 1) * cols] = (
            brecv[o].astype(F32) + erecv[q, :, at:at + cols].astype(F32)
        ).astype(BF16)

    for h in range(PIECES):
        @pl.when(z + 1 < n)
        def _():
            own_copy(1, h).wait_send()

        @pl.when(z > 0)
        def _():
            own_copy(0, h).wait_send()

    def drain(b, carry):
        for h in range(PIECES):
            @pl.when((b < z) & (z + 1 < n))
            def _():
                fwd_copy(b, h, z + 1).wait_send()

            @pl.when((b > z) & (z > 0))
            def _():
                fwd_copy(b, h, z - 1).wait_send()

        @pl.when(b != z)
        def _():
            remote(desc_ref.at[b], desc_v.at[z], desc_send.at[b], desc_recv.at[z], adapter=b).wait_send()
            delta_copy(b).wait_send()
            base_copy(b).wait_send()

        for j in range(1, tn):
            low_copy(b, j).wait_send()
            part_copy(b, j).wait_send()
        return carry

    lax.fori_loop(0, n, drain, 0)
    for j in range(1, tn):
        last_copy(j).wait_send()


def local(heads_out, out_weight, adapter_ids, shrink_weight, expand_weight):
    n = lax.axis_size("adapter")
    tn = lax.axis_size("tensor")
    rows, width = heads_out.shape
    local_count, rank = shrink_weight.shape[:2]
    cols = out_weight.shape[1]
    cap = max(2, max(rows // 8, (rows + n - 1) // n))
    mids = local_count * rank
    share = rows // tn

    any_spec = pl.BlockSpec(memory_space=pltpu.HBM)
    vmem_spec = pl.BlockSpec(memory_space=pltpu.VMEM)
    dma = pltpu.SemaphoreType.DMA
    return pl.pallas_call(
        functools.partial(kernel, n, tn, cap, rank, local_count),
        out_shape=jax.ShapeDtypeStruct((share, n * cols), BF16),
        in_specs=[any_spec] * 4 + [vmem_spec],
        out_specs=vmem_spec,
        scratch_shapes=[
            pltpu.VMEM((n, rows, width), BF16),
            pltpu.VMEM((width, cols), BF16),
            pltpu.VMEM((mids, width), BF16),
            pltpu.VMEM((mids, width), BF16),
            pltpu.VMEM((n, cap, rows + LANES), BF16),
            pltpu.VMEM((rows, n * cap), BF16),
            pltpu.VMEM((n, cap, rows + LANES), BF16),
            pltpu.VMEM((n, tn, cap, LANES), F32),
            pltpu.VMEM((n, tn, share, cols), BF16),
            pltpu.VMEM((n, tn, share, cols), BF16),
            pltpu.VMEM((n, cap, width), BF16),
            pltpu.VMEM((n, cap, width), BF16),
            pltpu.VMEM((n, share, cols), BF16),
            pltpu.VMEM((n, share, cols), BF16),
            pltpu.VMEM((tn, share, width), BF16),
            pltpu.VMEM((tn, share, width), BF16),
            dma((5,)),
            dma((2, PIECES)), dma((n, PIECES)), dma((n, PIECES)),
            dma((n,)), dma((n,)),
            dma((n, tn)), dma((n, tn)),
            dma((n, tn)), dma((n, tn)),
            dma((n,)), dma((n,)),
            dma((n,)), dma((n,)),
            dma((tn,)), dma((tn,)),
        ],
        compiler_params=pltpu.CompilerParams(
            collective_id=0, has_side_effects=True, vmem_limit_bytes=52 * 1024 * 1024
        ),
        cost_estimate=pl.CostEstimate(
            flops=2 * n * rows * width * cols, bytes_accessed=2 * width * (cols + 2 * mids), transcendentals=0
        ),
    )(
        heads_out,
        out_weight,
        shrink_weight.reshape(mids, width),
        expand_weight.reshape(mids, width),
        adapter_ids.reshape(1, rows),
    )


def solution(mesh):
    placed = (
        P(("groups", "adapter"), "tensor"),
        P("tensor", "adapter"),
        P(("groups", "adapter")),
        P(("groups", "adapter"), None, "tensor"),
        P(("groups", "adapter"), None, "tensor"),
    )
    return jax.shard_map(
        local,
        mesh=mesh,
        in_specs=placed,
        out_specs=P(("groups", "adapter", "tensor"), None),
        check_vma=False,
    )
```

```python
import functools

import jax
import jax.numpy as jnp
from jax import lax
from jax.experimental import pallas as pl
from jax.experimental.pallas import tpu as pltpu
from jax.sharding import PartitionSpec as P

MESH = pl.DeviceIdType.MESH
F32 = jnp.float32
BF16 = jnp.bfloat16
LANES = 128
PIECES = 2


def kernel(
    n, tn, cap, rank, count,
    x_ref, w_ref, s_ref, e_ref, ids_ref,
    out_ref,
    xall, w_v, s_v, e_v, desc_ref, undo, desc_v, low_v, psend, precv, dsend, drecv, bsend, brecv, esend, erecv,
    local_sem, xsend_sem, xfwd_sem, xrecv_sem, desc_send, desc_recv, low_send, low_recv,
    p_send, p_recv, d_send, d_recv, b_send, b_recv, e_send, e_recv,
):
    z = lax.axis_index("adapter")
    t = lax.axis_index("tensor")
    rows, width = x_ref.shape
    cols = w_ref.shape[1]
    share = rows // tn
    mids = s_ref.shape[0]
    groups = mids // LANES
    tile = min(512, cols)
    wtile = min(512, width)

    def remote(src, dst, ssem, rsem, **where):
        return pltpu.make_async_remote_copy(
            src_ref=src, dst_ref=dst, send_sem=ssem, recv_sem=rsem, device_id=where, device_id_type=MESH
        )

    def zpeer(j):
        return lax.rem(z + j, n)

    def tpeer(j):
        return lax.rem(t + j, tn)

    x_load = pltpu.make_async_copy(x_ref, xall.at[z], local_sem.at[0])
    s_load = pltpu.make_async_copy(s_ref, s_v, local_sem.at[1])
    w_load = pltpu.make_async_copy(w_ref, w_v, local_sem.at[2])
    e_load = pltpu.make_async_copy(e_ref, e_v, local_sem.at[3])
    x_load.start()
    s_load.start()
    w_load.start()
    e_load.start()

    barrier = pltpu.get_barrier_semaphore()
    for j in range(1, n):
        pl.semaphore_signal(barrier, inc=1, device_id={"adapter": zpeer(j)}, device_id_type=MESH)
    for j in range(1, tn):
        pl.semaphore_signal(barrier, inc=1, device_id={"tensor": tpeer(j)}, device_id_type=MESH)
    pl.semaphore_wait(barrier, n - 1 + tn - 1)

    def desc_copy(j):
        peer = zpeer(j)
        return remote(desc_ref.at[peer], desc_v.at[z], desc_send.at[peer], desc_recv.at[z], adapter=peer)

    piece = rows // PIECES

    def own_copy(side, h):
        part = pl.ds(h * piece, piece)
        return remote(
            x_ref.at[part], xall.at[z, part], xsend_sem.at[side, h], xrecv_sem.at[z, h],
            adapter=z + 1 if side else z - 1,
        )

    def fwd_copy(b, h, peer):
        part = pl.ds(h * piece, piece)
        return remote(xall.at[b, part], xall.at[b, part], xfwd_sem.at[b, h], xrecv_sem.at[b, h], adapter=peer)

    for h in range(PIECES):
        @pl.when(z + 1 < n)
        def _():
            own_copy(1, h).start()

        @pl.when(z > 0)
        def _():
            own_copy(0, h).start()

    ids = jnp.broadcast_to(ids_ref[...], (rows, rows))
    owner = jnp.zeros((rows, rows), jnp.int32)
    for o in range(1, n):
        owner = owner + (ids >= o * count).astype(jnp.int32)
    at = lax.broadcasted_iota(jnp.int32, (rows, rows), 0)
    lane = lax.broadcasted_iota(jnp.int32, (rows, rows), 1)
    owner_of = owner.astype(F32).T.astype(jnp.int32)
    place = jnp.sum(((owner == owner_of) & (at < lane)).astype(F32), axis=0, keepdims=True)
    target = owner[:1] * cap + place.astype(jnp.int32)
    slots = n * cap
    hits = jnp.broadcast_to(target, (slots, rows)) == lax.broadcasted_iota(jnp.int32, (slots, rows), 0)
    inside = (ids[:1] - owner[:1] * count + 1).astype(F32)
    which = jnp.sum(jnp.where(hits, jnp.broadcast_to(inside, (slots, rows)), 0.0), axis=1, keepdims=True) - 1.0
    table = hits.astype(F32)
    undo[...] = table.T.astype(BF16)
    desc_ref[:, :, pl.ds(0, rows)] = table.astype(BF16).reshape(n, cap, rows)
    desc_ref[:, :, pl.ds(rows, LANES)] = (
        jnp.broadcast_to(which, (slots, LANES)).astype(BF16).reshape(n, cap, LANES)
    )
    for j in range(1, n):
        desc_copy(j).start()
    desc_v[z] = desc_ref[z]

    inner = jnp.where(z > n - 1 - z, -1, 1)
    paired = jnp.minimum(z, n - 1 - z)

    def block_of(s):
        d = (s + 1) // 2
        near = jnp.where(s % 2 == 1, z + inner * d, z - inner * d)
        far = z + inner * (s - paired)
        return jnp.where(s <= 2 * paired, near, far)

    def low_copy(b, j):
        return remote(low_v.at[b, t], low_v.at[b, t], low_send.at[b, j], low_recv.at[b, t], tensor=tpeer(j))

    def part_copy(b, j):
        peer = tpeer(j)
        return remote(psend.at[b, peer], precv.at[b, t], p_send.at[b, j], p_recv.at[b, t], tensor=peer)

    def delta_copy(b):
        return remote(dsend.at[b], drecv.at[z], d_send.at[b], d_recv.at[z], adapter=b)

    def base_copy(b):
        return remote(bsend.at[b], brecv.at[z], b_send.at[b], b_recv.at[z], adapter=b)

    def landed(ref, sem):
        return remote(ref, ref, local_sem.at[4], sem, tensor=tpeer(1))

    def mask_of(b):
        kk = desc_v[b, :, pl.ds(rows, LANES)].astype(F32)
        half = lax.broadcasted_iota(jnp.int32, (cap, LANES), 1) // rank
        return [kk == (half + g * (LANES // rank)).astype(F32) for g in range(groups)]

    def take(b, h):
        part = xall.at[b, pl.ds(h * piece, piece)]
        landed(part, xrecv_sem.at[b, h]).wait_recv()

        @pl.when((b < z) & (z + 1 < n))
        def _():
            fwd_copy(b, h, z + 1).start()

        @pl.when((b > z) & (z > 0))
        def _():
            fwd_copy(b, h, z - 1).start()

    def held(s):
        return (s > 0) & (s <= 2 * paired)

    def first(s):
        b = block_of(s)

        @pl.when(s == 0)
        def _():
            x_load.wait()
            s_load.wait()

        @pl.when(s > 0)
        def _():
            for h in range(PIECES):
                @pl.when((s > 2 * paired) | (s % 2 == 1))
                def _():
                    take(b, h)

                @pl.when((s < 2 * paired) & (s % 2 == 1))
                def _():
                    take(block_of(s + 1), h)

            landed(desc_v.at[b], desc_recv.at[b]).wait_recv()

        picked = jnp.dot(
            desc_v[b, :, pl.ds(0, rows)], xall[b], preferred_element_type=F32
        ).astype(BF16)
        shrunk = lax.dot_general(
            picked, s_v[...], (((1,), (1,)), ((), ())), preferred_element_type=F32
        )
        fold = jnp.zeros((cap, LANES), F32)
        for g, hit in enumerate(mask_of(b)):
            fold = fold + jnp.where(hit, shrunk[:, g * LANES:(g + 1) * LANES], 0.0)
        low_v[b, t] = fold
        for j in range(1, tn):
            low_copy(b, j).start()

        @pl.when(s == 0)
        def _():
            w_load.wait()

        def column(i, carry):
            span = pl.ds(pl.multiple_of(i * tile, tile), tile)
            part = jnp.dot(xall[b], w_v[:, span], preferred_element_type=F32)
            for q in range(tn):
                psend[b, q, :, span] = part[q * share:(q + 1) * share].astype(BF16)
            for j in range(1, tn):
                peer = tpeer(j)
                remote(
                    psend.at[b, peer, :, span], precv.at[b, t, :, span],
                    p_send.at[b, j], p_recv.at[b, t], tensor=peer,
                ).start()
            return carry

        lax.fori_loop(0, cols // tile, column, 0)

        @pl.when(s == 0)
        def _():
            e_load.wait()

    def delta_part(s):
        b = block_of(s)
        for j in range(1, tn):
            peer = tpeer(j)
            landed(low_v.at[b, peer], low_recv.at[b, peer]).wait_recv()
        total = low_v[b, 0]
        for q in range(1, tn):
            total = total + low_v[b, q]
        low = 0.5 * total
        routed = jnp.concatenate([jnp.where(hit, low, 0.0) for hit in mask_of(b)], axis=1).astype(BF16)
        delta = jnp.dot(routed, e_v[...], preferred_element_type=F32).astype(BF16)

        @pl.when(b == z)
        def _():
            drecv[b] = delta

        @pl.when(b != z)
        def _():
            dsend[b] = delta

        @pl.when((b != z) & jnp.logical_not(held(s)))
        def _():
            delta_copy(b).start()

    def base_part(s):
        b = block_of(s)
        for j in range(1, tn):
            peer = tpeer(j)
            landed(precv.at[b, peer], p_recv.at[b, peer]).wait_recv()
        acc = psend[b, t].astype(F32)
        for j in range(1, tn):
            acc = acc + precv[b, tpeer(j)].astype(F32)
        base = acc.astype(BF16)

        @pl.when(b == z)
        def _():
            brecv[b] = base

        @pl.when(b != z)
        def _():
            bsend[b] = base

        @pl.when((b != z) & jnp.logical_not(held(s)))
        def _():
            base_copy(b).start()

    last = max(n - 1, 3)

    def step(s, carry):
        @pl.when(s < n)
        def _():
            first(s)

        @pl.when((s == last) & (paired > 0))
        def _():
            delta_copy(block_of(1)).start()
            delta_copy(block_of(2)).start()
            base_copy(block_of(1)).start()

        @pl.when(s < n)
        def _():
            delta_part(s)

        @pl.when(s > 0)
        def _():
            base_part(s - 1)

        return carry

    def release_all(s, carry):
        @pl.when(held(s))
        def _():
            @pl.when(s > 2)
            def _():
                delta_copy(block_of(s)).start()

            @pl.when(s > 1)
            def _():
                base_copy(block_of(s)).start()

        return carry

    lax.fori_loop(0, n + 1, step, 0)
    lax.fori_loop(2, n, release_all, 0)

    for j in range(1, n):
        peer = zpeer(j)
        landed(drecv.at[peer], d_recv.at[peer]).wait_recv()

    def spread(i, carry):
        span = pl.ds(pl.multiple_of(i * wtile, wtile), wtile)
        flat = drecv[:, :, span].reshape(n * cap, wtile)
        mine = jnp.dot(undo[...], flat, preferred_element_type=F32).astype(BF16)
        for q in range(tn):
            esend[q, :, span] = mine[q * share:(q + 1) * share]
        for j in range(1, tn):
            peer = tpeer(j)
            remote(
                esend.at[peer, :, span], erecv.at[t, :, span], e_send.at[j], e_recv.at[t], tensor=peer
            ).start()
        return carry

    lax.fori_loop(0, width // wtile, spread, 0)

    def last_copy(j):
        peer = tpeer(j)
        return remote(esend.at[peer], erecv.at[t], e_send.at[j], e_recv.at[t], tensor=peer)

    erecv[t] = esend[t]
    for j in range(1, n):
        peer = zpeer(j)
        landed(brecv.at[peer], b_recv.at[peer]).wait_recv()
    for j in range(1, tn):
        peer = tpeer(j)
        landed(erecv.at[peer], e_recv.at[peer]).wait_recv()
    for o in range(n):
        q, at = (o * cols) // width, (o * cols) % width
        out_ref[:, o * cols:(o + 1) * cols] = (
            brecv[o].astype(F32) + erecv[q, :, at:at + cols].astype(F32)
        ).astype(BF16)

    for h in range(PIECES):
        @pl.when(z + 1 < n)
        def _():
            own_copy(1, h).wait_send()

        @pl.when(z > 0)
        def _():
            own_copy(0, h).wait_send()

    def drain(b, carry):
        for h in range(PIECES):
            @pl.when((b < z) & (z + 1 < n))
            def _():
                fwd_copy(b, h, z + 1).wait_send()

            @pl.when((b > z) & (z > 0))
            def _():
                fwd_copy(b, h, z - 1).wait_send()

        @pl.when(b != z)
        def _():
            remote(desc_ref.at[b], desc_v.at[z], desc_send.at[b], desc_recv.at[z], adapter=b).wait_send()
            delta_copy(b).wait_send()
            base_copy(b).wait_send()

        for j in range(1, tn):
            low_copy(b, j).wait_send()
            part_copy(b, j).wait_send()
        return carry

    lax.fori_loop(0, n, drain, 0)
    for j in range(1, tn):
        last_copy(j).wait_send()


def local(heads_out, out_weight, adapter_ids, shrink_weight, expand_weight):
    n = lax.axis_size("adapter")
    tn = lax.axis_size("tensor")
    rows, width = heads_out.shape
    local_count, rank = shrink_weight.shape[:2]
    cols = out_weight.shape[1]
    cap = max(2, max(rows // 8, (rows + n - 1) // n))
    mids = local_count * rank
    share = rows // tn

    any_spec = pl.BlockSpec(memory_space=pltpu.HBM)
    vmem_spec = pl.BlockSpec(memory_space=pltpu.VMEM)
    dma = pltpu.SemaphoreType.DMA
    return pl.pallas_call(
        functools.partial(kernel, n, tn, cap, rank, local_count),
        out_shape=jax.ShapeDtypeStruct((share, n * cols), BF16),
        in_specs=[any_spec] * 4 + [vmem_spec],
        out_specs=vmem_spec,
        scratch_shapes=[
            pltpu.VMEM((n, rows, width), BF16),
            pltpu.VMEM((width, cols), BF16),
            pltpu.VMEM((mids, width), BF16),
            pltpu.VMEM((mids, width), BF16),
            pltpu.VMEM((n, cap, rows + LANES), BF16),
            pltpu.VMEM((rows, n * cap), BF16),
            pltpu.VMEM((n, cap, rows + LANES), BF16),
            pltpu.VMEM((n, tn, cap, LANES), F32),
            pltpu.VMEM((n, tn, share, cols), BF16),
            pltpu.VMEM((n, tn, share, cols), BF16),
            pltpu.VMEM((n, cap, width), BF16),
            pltpu.VMEM((n, cap, width), BF16),
            pltpu.VMEM((n, share, cols), BF16),
            pltpu.VMEM((n, share, cols), BF16),
            pltpu.VMEM((tn, share, width), BF16),
            pltpu.VMEM((tn, share, width), BF16),
            dma((5,)),
            dma((2, PIECES)), dma((n, PIECES)), dma((n, PIECES)),
            dma((n,)), dma((n,)),
            dma((n, tn)), dma((n, tn)),
            dma((n, tn)), dma((n, tn)),
            dma((n,)), dma((n,)),
            dma((n,)), dma((n,)),
            dma((tn,)), dma((tn,)),
        ],
        compiler_params=pltpu.CompilerParams(
            collective_id=0, has_side_effects=True, vmem_limit_bytes=52 * 1024 * 1024
        ),
        cost_estimate=pl.CostEstimate(
            flops=2 * n * rows * width * cols, bytes_accessed=2 * width * (cols + 2 * mids), transcendentals=0
        ),
    )(
        heads_out,
        out_weight,
        shrink_weight.reshape(mids, width),
        expand_weight.reshape(mids, width),
        adapter_ids.reshape(1, rows),
    )


def solution(mesh):
    placed = (
        P(("groups", "adapter"), "tensor"),
        P("tensor", "adapter"),
        P(("groups", "adapter")),
        P(("groups", "adapter"), None, "tensor"),
        P(("groups", "adapter"), None, "tensor"),
    )
    return jax.shard_map(
        local,
        mesh=mesh,
        in_specs=placed,
        out_specs=P(("groups", "adapter", "tensor"), None),
        check_vma=False,
    )
```
